32 devices in a mesh: group: 2 (over y), snp: 4 (over x, core), ind: 4 (over z).
Axes of the slice: x: 2, y: 2, z: 4, core: 2. Of those that a mesh axis runs over, the one named last changes fastest.
Arguments:
- genotypes: int32 [8192, 8192], P(('group', 'ind'), 'snp'), parts along dimension 0, may hold values from 0 to 255, as said below
- ancestry: float32 [64, 32768], P(None, ('group', 'ind')), parts along dimension 1, may hold values from 0 to 1, as said below
- frequency: float32 [64, 16384], P(None, ('group', 'snp')), parts along dimension 1, may hold values from 0.05 to 0.95
Outputs:
- ancestry_new: float32 [64, 32768], P(None, ('group', 'ind')), parts along dimension 1
- frequency_new: float32 [64, 16384], P(None, ('group', 'snp')), parts along dimension 1
The draws below stay inside these ranges and needn't reach their ends.
There are 2 independent parts, one for each index of `group`. The reference program is written for one: setup_inputs(seed, part) draws one part's arguments, and reference() takes and returns one part's arrays. A program takes and returns all parts, laid end to end along the dimension named above; each array names one. Nothing has to cross between parts.
Inputs may be any that keep to these rules, and one draw needn't show every extreme that they name: `genotypes`: each word holds four 2-bit codes as in the first step; every code is 0, 1, 2 (allele count) or 3 (missing). `ancestry`: entries are positive and each individual's column sums to one.
All inputs are finite; a program needn't handle non-finite values.
Results may differ from the reference program's by a relative error of at most 0.0003.
Values sent between devices are 32-bit elements; how exact they have to be, the bound alone decides.
A program may use at most 64 MiB of HBM per device.

```python
import jax
import jax.numpy as jnp
from jax import lax

K = 64
IND_DEV = 4096
SNP_DEV = 2048
INDS = 16384
SNPS = 8192
N_SNP = 4
N_IND = 4


def shared_tables(key):
    cohort_key = jax.random.fold_in(key, 101)
    allele_key = jax.random.fold_in(key, 102)
    cohorts = INDS // (IND_DEV // 2)
    cohort_pops = jax.random.randint(cohort_key, (cohorts, 3), 0, K)
    allele_codes = jax.random.randint(allele_key, (K, SNPS), 0, 3)
    return (cohort_pops, allele_codes)


def draw_genotypes(key, part):
    cohort_pops, allele_codes = shared_tables(key)
    key = jax.random.fold_in(key, 7)
    segments = SNPS // SNP_DEV
    picked = jax.random.randint(jax.random.fold_in(key, 1), (INDS, segments), 0, 3)
    member = jnp.arange(INDS, dtype=jnp.int32) // (IND_DEV // 2)
    source = jnp.take_along_axis(cohort_pops[member], picked, axis=1)
    weights = 4 ** jnp.arange(4, dtype=jnp.int32)
    row_ids = jnp.arange(IND_DEV, dtype=jnp.int32)
    col_ids = jnp.arange(SNPS, dtype=jnp.int32)
    forced = (row_ids % (IND_DEV // 4) == 0)[:, None] & (col_ids == 0)[None, :]

    def one_block(block):
        rows = lax.dynamic_slice_in_dim(source, block * IND_DEV, IND_DEV, 0)
        spread = jnp.repeat(rows, SNP_DEV, axis=1)
        allele = jnp.take_along_axis(allele_codes, spread, axis=0)
        block_key = jax.random.fold_in(key, block + 2)
        noise = jax.random.randint(jax.random.fold_in(block_key, 1), (IND_DEV, SNPS), 0, 20)
        random_codes = jax.random.randint(jax.random.fold_in(block_key, 2), (IND_DEV, SNPS), 0, 3)
        values = jnp.where(noise < 3, random_codes, allele)
        values = jnp.where(noise == 19, 3, values)
        values = jnp.where(forced & (block == 0), 3, values)
        stacked = values.reshape(4, IND_DEV // 4, SNPS)
        return jnp.sum(stacked * weights[:, None, None], axis=0).astype(jnp.int32)
    words = lax.map(one_block, jnp.arange(INDS // IND_DEV, dtype=jnp.int32))
    return words.reshape(INDS // 4, SNPS)


def draw_ancestry(key, part):
    cohort_pops, allele_codes = shared_tables(key)
    key = jax.random.fold_in(key, 8)
    member = jnp.arange(INDS, dtype=jnp.int32) // (IND_DEV // 2)
    mine = cohort_pops[member]
    levels = jnp.arange(K, dtype=jnp.int32)
    belongs = jnp.any(levels[:, None, None] == mine[None], axis=2).astype(jnp.float32)
    spread = jnp.exp(0.7 * jax.random.normal(key, (K, INDS), jnp.float32))
    boost = 3.0
    raw = spread * (1.0 + boost * belongs)
    return raw / jnp.sum(raw, axis=0, keepdims=True)


def draw_frequency(key, part):
    cohort_pops, allele_codes = shared_tables(key)
    key = jax.random.fold_in(key, 9)
    jitter = 0.03 * jnp.tanh(jax.random.normal(key, (K, SNPS), jnp.float32))
    return 0.08 + 0.42 * allele_codes.astype(jnp.float32) + jitter


def setup_inputs(seed: int = 0, part: int = 0) -> dict:
    seeds = jax.random.split(jax.random.key(seed), 4)
    part_keys = jax.random.split(jax.random.fold_in(seeds[3], part), 4)
    genotypes = draw_genotypes(jax.random.fold_in(jax.random.fold_in(seeds[3], part), 71), part)
    ancestry = draw_ancestry(jax.random.fold_in(jax.random.fold_in(seeds[3], part), 71), part)
    frequency = draw_frequency(jax.random.fold_in(jax.random.fold_in(seeds[3], part), 71), part)
    return dict(genotypes=genotypes, ancestry=ancestry, frequency=frequency)


def reference(genotypes, ancestry, frequency):
    shifts = 2 * jnp.arange(4, dtype=jnp.int32)
    q_half = ancestry.astype(jnp.bfloat16)
    f_half = frequency.astype(jnp.bfloat16)
    rest_half = (1.0 - frequency).astype(jnp.bfloat16)

    def block(carry, index):
        start = (index * SNP_DEV).astype(jnp.int32)
        words = lax.dynamic_slice_in_dim(genotypes, start, SNP_DEV, 1)
        words = words.reshape(N_IND, IND_DEV // 4, SNP_DEV)
        codes = ((words[:, None] >> shifts[None, :, None, None]) & 3).reshape(INDS, SNP_DEV)
        f_block = lax.dynamic_slice_in_dim(f_half, start, SNP_DEV, 1)
        rest_block = lax.dynamic_slice_in_dim(rest_half, start, SNP_DEV, 1)
        mixed = jnp.dot(q_half.T, f_block, preferred_element_type=jnp.float32)
        seen = codes < 3
        counts = codes.astype(jnp.float32)
        ratio_a = jnp.where(seen, counts / mixed, 0.0).astype(jnp.bfloat16)
        ratio_b = jnp.where(seen, (2.0 - counts) / (1.0 - mixed), 0.0).astype(jnp.bfloat16)
        stat = carry + jnp.dot(f_block, ratio_a.T, preferred_element_type=jnp.float32)
        stat = stat + jnp.dot(rest_block, ratio_b.T, preferred_element_type=jnp.float32)
        allele_a = jnp.dot(q_half, ratio_a, preferred_element_type=jnp.float32)
        allele_b = jnp.dot(q_half, ratio_b, preferred_element_type=jnp.float32)
        return stat, (allele_a, allele_b)

    stat, (allele_a, allele_b) = lax.scan(block, jnp.zeros((K, INDS), jnp.float32), jnp.arange(N_SNP, dtype=jnp.int32))
    allele_a = allele_a.transpose(1, 0, 2).reshape(K, SNPS)
    allele_b = allele_b.transpose(1, 0, 2).reshape(K, SNPS)
    weighted = ancestry * stat
    ancestry_new = K * weighted / jnp.sum(weighted, axis=0, keepdims=True)
    upper_part = frequency * allele_a
    frequency_new = upper_part / (upper_part + (1.0 - frequency) * allele_b)
    return ancestry_new, frequency_new
```

```python
import functools

import jax
import jax.numpy as jnp
from jax import lax
from jax.experimental import pallas as pl
from jax.experimental.pallas import tpu as pltpu
from jax.sharding import PartitionSpec as P

F32 = jnp.float32
BF16 = jnp.bfloat16
SNP_BLOCK = 512
WORD_BLOCK = 256
MESH = pl.DeviceIdType.MESH


def product(left, right, left_dim, right_dim):
    return lax.dot_general(
        left, right, (((left_dim,), (right_dim,)), ((), ())), preferred_element_type=F32
    )


def remote(src, dst, sems, recv, index, target):
    return pltpu.make_async_remote_copy(
        src_ref=src,
        dst_ref=dst,
        send_sem=sems.at[index],
        recv_sem=recv.at[index],
        device_id=target,
        device_id_type=MESH,
    )


def kernel(
    n_ind, n_snp, chunks,
    words_ref, anc_ref, freq_ref, anc_out, freq_out,
    words, q_half, q_turned, f_half, rest_half, allele, allele_in, fresh,
    stat, stat_one, stat_two, updated,
    word_sem, allele_send, allele_recv, fresh_send, fresh_recv, fresh_own,
    one_send, one_recv, two_send, two_recv, new_send, new_recv, pass_send, pass_recv, own_sem,
):
    k, people = anc_ref.shape
    columns = freq_ref.shape[1]
    height = words_ref.shape[0]
    blocks = columns // SNP_BLOCK
    tiles = height // WORD_BLOCK
    rows = k // n_ind
    half = n_snp // 2
    span = people // (chunks * n_snp)
    pieces = WORD_BLOCK // span
    per_chunk = tiles // chunks

    me = lax.axis_index("ind")
    here = lax.axis_index("snp")
    core = lax.rem(here, 2)
    place = here // 2
    mate = {"snp": here + 1 - 2 * core}

    def ind_peer(step):
        return lax.rem(me + step, n_ind)

    def place_peer(step):
        return lax.rem(place + step, half)

    def place_id(step):
        return {"snp": place_peer(step) * 2 + core}

    def word_copy(block, tile):
        start = block * SNP_BLOCK
        if not isinstance(start, int):
            start = pl.multiple_of(start, SNP_BLOCK)
        return pltpu.make_async_copy(
            words_ref.at[pl.ds(tile * WORD_BLOCK, WORD_BLOCK), pl.ds(start, SNP_BLOCK)],
            words.at[block, pl.ds(tile * WORD_BLOCK, WORD_BLOCK)],
            word_sem.at[block, tile],
        )

    for block in range(blocks):
        for tile in range(tiles):
            word_copy(block, tile).start()

    barrier = pltpu.get_barrier_semaphore()
    for step in range(1, n_ind):
        pl.semaphore_signal(barrier, 1, device_id={"ind": ind_peer(step)}, device_id_type=MESH)
    for step in range(1, half):
        pl.semaphore_signal(barrier, 1, device_id=place_id(step), device_id_type=MESH)
    pl.semaphore_signal(barrier, 1, device_id=mate, device_id_type=MESH)

    for block in range(blocks):
        cols = pl.ds(block * SNP_BLOCK, SNP_BLOCK)
        f_part = freq_ref[:, cols]
        f_half[block] = f_part.astype(BF16)
        rest_half[block] = (1.0 - f_part).astype(BF16)
    for run in range(people // WORD_BLOCK):
        cols = pl.ds(run * WORD_BLOCK, WORD_BLOCK)
        part = anc_ref[:, cols].astype(BF16)
        q_half[:, cols] = part
        q_turned[cols, :] = part.T
    stat[...] = jnp.zeros_like(stat)

    def tile_terms(block, tile):
        word_copy(block, tile).wait()
        f_part = f_half[block]
        rest_part = rest_half[block]
        packed = words[block, pl.ds(tile * WORD_BLOCK, WORD_BLOCK), :].astype(jnp.int16)
        for t in range(4):
            start = t * height + tile * WORD_BLOCK
            mixed = product(q_turned[pl.ds(start, WORD_BLOCK), :], f_part, 1, 0)
            inv_a = pltpu.reciprocal(mixed, approx=True).astype(BF16)
            inv_b = pltpu.reciprocal(1.0 - mixed, approx=True).astype(BF16)
            code = packed & jnp.int16(3 << (2 * t))
            one = code == jnp.int16(1 << (2 * t))
            two = code == jnp.int16(2 << (2 * t))
            none = code == jnp.int16(0)
            zero = jnp.zeros_like(inv_a)
            ratio_a = jnp.where(one, inv_a, jnp.where(two, inv_a + inv_a, zero))
            ratio_b = jnp.where(one, inv_b, jnp.where(none, inv_b + inv_b, zero))
            term = product(f_part, ratio_a, 1, 1) + product(rest_part, ratio_b, 1, 1)
            for piece in range(pieces):
                owner = ((tile % per_chunk) * 4 + t) * pieces + piece
                stat[tile // per_chunk, owner % 2, owner // 2] += term[:, piece * span:(piece + 1) * span]
            q_part = q_half[:, pl.ds(start, WORD_BLOCK)]
            sum_a = product(q_part, ratio_a, 1, 0)
            sum_b = product(q_part, ratio_b, 1, 0)
            if tile == 0 and t == 0:
                allele[block, 0] = sum_a
                allele[block, 1] = sum_b
            else:
                allele[block, 0] += sum_a
                allele[block, 1] += sum_b

    def own_rows(owner):
        return pl.ds(pl.multiple_of(owner * rows, rows), rows)

    def allele_copy(block, step):
        peer = ind_peer(step)
        return remote(
            allele.at[block, :, own_rows(peer)], allele_in.at[block, step - 1],
            allele_send, allele_recv, (block, step - 1), {"ind": peer},
        )

    def fresh_place(block):
        start = block * SNP_BLOCK
        if not isinstance(start, int):
            start = pl.multiple_of(start, SNP_BLOCK)
        return freq_out.at[own_rows(me), pl.ds(start, SNP_BLOCK)]

    def fresh_copy(block, step):
        return remote(
            fresh.at[block], fresh_place(block),
            fresh_send, fresh_recv, (block, step - 1), {"ind": ind_peer(step)},
        )

    def fresh_keep(block):
        return pltpu.make_async_copy(fresh.at[block], fresh_place(block), fresh_own.at[block])

    def allele_start(block):
        for step in range(1, n_ind):
            allele_copy(block, step).start()

    def allele_finish(block):
        total = allele[block, :, own_rows(me), :]
        for step in range(1, n_ind):
            allele_copy(block, step).wait_recv()
            total = total + allele_in[block, step - 1]
        start = block * SNP_BLOCK
        if not isinstance(start, int):
            start = pl.multiple_of(start, SNP_BLOCK)
        current = freq_ref[own_rows(me), pl.ds(start, SNP_BLOCK)]
        upper = current * total[0]
        fresh[block] = upper / (upper + (1.0 - current) * total[1])
        for step in range(1, n_ind):
            fresh_copy(block, step).start()
        fresh_keep(block).start()

    def one_copy(chunk):
        return remote(
            stat.at[chunk, 1 - core], stat_one.at[chunk], one_send, one_recv, chunk, mate
        )

    def two_copy(chunk, step):
        return remote(
            stat.at[chunk, core, place_peer(step)], stat_two.at[chunk, step - 1],
            two_send, two_recv, (chunk, step - 1), place_id(step),
        )

    def individuals(chunk, owner):
        run = owner // pieces
        tile = chunk * per_chunk + run // 4
        start = lax.rem(run, 4) * height + tile * WORD_BLOCK + lax.rem(owner, pieces) * span
        return pl.ds(pl.multiple_of(start, span), span)

    def new_copy(chunk, step):
        return remote(
            updated.at[chunk], anc_out.at[:, individuals(chunk, here)],
            new_send, new_recv, (chunk, step - 1), place_id(step),
        )

    def new_mate(chunk):
        return remote(
            updated.at[chunk], anc_out.at[:, individuals(chunk, here)],
            new_send, new_recv, (chunk, half - 1), mate,
        )

    def new_keep(chunk):
        return pltpu.make_async_copy(
            updated.at[chunk], anc_out.at[:, individuals(chunk, here)], own_sem.at[chunk]
        )

    def pass_copy(chunk, step):
        owner = lax.rem(place + half - step, half) * 2 + core
        part = anc_out.at[:, individuals(chunk, owner)]
        return remote(part, part, pass_send, pass_recv, (chunk, step - 1), mate)

    def stat_send(chunk):
        one_copy(chunk).start()

    def stat_pair(chunk):
        one_copy(chunk).wait()
        for step in range(1, half):
            peer = place_peer(step)
            stat[chunk, core, peer] += stat_one[chunk, peer]
            two_copy(chunk, step).start()
        stat[chunk, core, place] += stat_one[chunk, place]

    def stat_new(chunk):
        total = stat[chunk, core, place]
        for step in range(1, half):
            two_copy(chunk, step).wait_recv()
            total = total + stat_two[chunk, step - 1]
        weighted = anc_ref[:, individuals(chunk, here)] * total
        updated[chunk] = k * weighted / jnp.sum(weighted, axis=0, keepdims=True)
        for step in range(1, half):
            new_copy(chunk, step).start()
        new_mate(chunk).start()
        new_keep(chunk).start()

    def stat_pass(chunk):
        for step in range(1, half):
            new_copy(chunk, step).wait_recv()
            pass_copy(chunk, step).start()

    stages = (stat_send, stat_pair, stat_new, stat_pass)

    def tick(now):
        for stage, act in enumerate(stages):
            if 0 <= now - stage < chunks:
                act(now - stage)

    def sweep(block, carry):
        for tile in range(tiles):
            tile_terms(block, tile)

        @pl.when(block == 0)
        def _():
            pl.semaphore_wait(barrier, n_ind - 1 + half)

        allele_start(block)

        @pl.when(block > 0)
        def _():
            allele_finish(block - 1)

        return carry

    last = blocks - 1
    lax.fori_loop(0, last, sweep, 0)
    for tile in range(tiles):
        tile_terms(last, tile)
        if tile == tiles - 1:
            allele_start(last)
        if (tile + 1) % per_chunk == 0:
            tick(tile // per_chunk)
    allele_finish(last - 1)
    tick(chunks)
    tick(chunks + 1)
    allele_finish(last)
    tick(chunks + 2)

    for chunk in range(chunks):
        for step in range(1, half):
            two_copy(chunk, step).wait_send()
            new_copy(chunk, step).wait_send()
            pass_copy(chunk, step).wait()
        new_mate(chunk).wait()
        new_keep(chunk).wait()
    for block in range(blocks):
        for step in range(1, n_ind):
            allele_copy(block, step).wait_send()
            fresh_copy(block, step).wait()
        fresh_keep(block).wait()


def on_device(n_ind, n_snp, genotypes, ancestry, frequency):
    k, people = ancestry.shape
    columns = frequency.shape[1]
    height = genotypes.shape[0]
    blocks = columns // SNP_BLOCK
    tiles = height // WORD_BLOCK
    half = n_snp // 2
    chunks = min(tiles, people // (n_snp * 128))
    span = people // (chunks * n_snp)
    rows = k // n_ind
    dma = pltpu.SemaphoreType.DMA
    vmem = pl.BlockSpec(memory_space=pltpu.VMEM)
    anywhere = pl.BlockSpec(memory_space=pl.ANY)
    return pl.pallas_call(
        functools.partial(kernel, n_ind, n_snp, chunks),
        out_shape=(
            jax.ShapeDtypeStruct(ancestry.shape, F32),
            jax.ShapeDtypeStruct(frequency.shape, F32),
        ),
        in_specs=[anywhere, vmem, vmem],
        out_specs=(anywhere, anywhere),
        scratch_shapes=[
            pltpu.VMEM((blocks, height, SNP_BLOCK), jnp.int32),
            pltpu.VMEM((k, people), BF16),
            pltpu.VMEM((people, k), BF16),
            pltpu.VMEM((blocks, k, SNP_BLOCK), BF16),
            pltpu.VMEM((blocks, k, SNP_BLOCK), BF16),
            pltpu.VMEM((blocks, 2, k, SNP_BLOCK), F32),
            pltpu.VMEM((blocks, n_ind - 1, 2, rows, SNP_BLOCK), F32),
            pltpu.VMEM((blocks, rows, SNP_BLOCK), F32),
            pltpu.VMEM((chunks, 2, half, k, span), F32),
            pltpu.VMEM((chunks, half, k, span), F32),
            pltpu.VMEM((chunks, half - 1, k, span), F32),
            pltpu.VMEM((chunks, k, span), F32),
            dma((blocks, tiles)),
            dma((blocks, n_ind - 1)),
            dma((blocks, n_ind - 1)),
            dma((blocks, n_ind - 1)),
            dma((blocks, n_ind - 1)),
            dma((blocks,)),
            dma((chunks,)),
            dma((chunks,)),
            dma((chunks, half - 1)),
            dma((chunks, half - 1)),
            dma((chunks, half)),
            dma((chunks, half)),
            dma((chunks, half - 1)),
            dma((chunks, half - 1)),
            dma((chunks,)),
        ],
        compiler_params=pltpu.CompilerParams(
            collective_id=0, has_side_effects=True, vmem_limit_bytes=48 * 2**20
        ),
        name="admixture_step",
    )(genotypes, ancestry, frequency)


def solution(mesh):
    placed = (P(("group", "ind"), "snp"), P(None, ("group", "ind")), P(None, ("group", "snp")))
    return jax.shard_map(
        functools.partial(on_device, mesh.shape["ind"], mesh.shape["snp"]),
        mesh=mesh,
        in_specs=placed,
        out_specs=(P(None, ("group", "ind")), P(None, ("group", "snp"))),
        check_vma=False,
    )
```

```python
import functools

import jax
import jax.numpy as jnp
from jax import lax
from jax.experimental import pallas as pl
from jax.experimental.pallas import tpu as pltpu
from jax.sharding import PartitionSpec as P

F32 = jnp.float32
BF16 = jnp.bfloat16
SNP_BLOCK = 512
WORD_BLOCK = 256
MESH = pl.DeviceIdType.MESH


def product(left, right, left_dim, right_dim):
    return lax.dot_general(
        left, right, (((left_dim,), (right_dim,)), ((), ())), preferred_element_type=F32
    )


def remote(src, dst, sems, recv, index, target):
    return pltpu.make_async_remote_copy(
        src_ref=src,
        dst_ref=dst,
        send_sem=sems.at[index],
        recv_sem=recv.at[index],
        device_id=target,
        device_id_type=MESH,
    )


def kernel(
    n_ind, n_snp, chunks,
    words_ref, anc_ref, freq_ref, anc_out, freq_out,
    words, q_half, q_turned, f_half, rest_half, allele, allele_one, allele_two, allele_in, fresh,
    stat, stat_one, stat_two, updated,
    word_sem, half_send, half_recv, allele_send, allele_recv, fresh_send, fresh_recv, fresh_own,
    hand_send, hand_recv, direct_send, direct_recv, last_send, last_recv,
    one_send, one_recv, two_send, two_recv, new_send, new_recv, pass_send, pass_recv, own_sem,
):
    k, people = anc_ref.shape
    columns = freq_ref.shape[1]
    height = words_ref.shape[0]
    blocks = columns // SNP_BLOCK
    tiles = height // WORD_BLOCK
    last = blocks - 1
    rows = k // n_ind
    half = n_snp // 2
    depth = n_ind // 2
    side_rows = k // 2
    span = people // (chunks * n_snp)
    pieces = WORD_BLOCK // span
    per_chunk = tiles // chunks

    me = lax.axis_index("ind")
    side = lax.rem(me, 2)
    level = me // 2
    neighbour = {"ind": me + 1 - 2 * side}
    here = lax.axis_index("snp")
    core = lax.rem(here, 2)
    place = here // 2
    mate = {"snp": here + 1 - 2 * core}

    def ind_peer(step):
        return lax.rem(me + step, n_ind)

    def level_peer(step):
        return lax.rem(level + step, depth)

    def level_id(step):
        return {"ind": level_peer(step) * 2 + side}

    def place_peer(step):
        return lax.rem(place + step, half)

    def place_id(step):
        return {"snp": place_peer(step) * 2 + core}

    def word_copy(block, tile):
        start = block * SNP_BLOCK
        if not isinstance(start, int):
            start = pl.multiple_of(start, SNP_BLOCK)
        return pltpu.make_async_copy(
            words_ref.at[pl.ds(tile * WORD_BLOCK, WORD_BLOCK), pl.ds(start, SNP_BLOCK)],
            words.at[block, pl.ds(tile * WORD_BLOCK, WORD_BLOCK)],
            word_sem.at[block, tile],
        )

    for block in range(blocks):
        for tile in range(tiles):
            word_copy(block, tile).start()

    barrier = pltpu.get_barrier_semaphore()
    for step in range(1, n_ind):
        pl.semaphore_signal(barrier, 1, device_id={"ind": ind_peer(step)}, device_id_type=MESH)
    for step in range(1, half):
        pl.semaphore_signal(barrier, 1, device_id=place_id(step), device_id_type=MESH)
    pl.semaphore_signal(barrier, 1, device_id=mate, device_id_type=MESH)

    for block in range(blocks):
        cols = pl.ds(block * SNP_BLOCK, SNP_BLOCK)
        f_part = freq_ref[:, cols]
        f_half[block] = f_part.astype(BF16)
        rest_half[block] = (1.0 - f_part).astype(BF16)
    for run in range(people // WORD_BLOCK):
        cols = pl.ds(run * WORD_BLOCK, WORD_BLOCK)
        part = anc_ref[:, cols].astype(BF16)
        q_half[:, cols] = part
        q_turned[cols, :] = part.T
    stat[...] = jnp.zeros_like(stat)

    def tile_terms(block, tile):
        word_copy(block, tile).wait()
        f_part = f_half[block]
        rest_part = rest_half[block]
        packed = words[block, pl.ds(tile * WORD_BLOCK, WORD_BLOCK), :].astype(jnp.int16)
        for t in range(4):
            start = t * height + tile * WORD_BLOCK
            mixed = product(q_turned[pl.ds(start, WORD_BLOCK), :], f_part, 1, 0)
            inv_a = pltpu.reciprocal(mixed, approx=True).astype(BF16)
            inv_b = pltpu.reciprocal(1.0 - mixed, approx=True).astype(BF16)
            code = packed & jnp.int16(3 << (2 * t))
            one = code == jnp.int16(1 << (2 * t))
            two = code == jnp.int16(2 << (2 * t))
            none = code == jnp.int16(0)
            zero = jnp.zeros_like(inv_a)
            ratio_a = jnp.where(one, inv_a, jnp.where(two, inv_a + inv_a, zero))
            ratio_b = jnp.where(one, inv_b, jnp.where(none, inv_b + inv_b, zero))
            term = product(f_part, ratio_a, 1, 1) + product(rest_part, ratio_b, 1, 1)
            for piece in range(pieces):
                owner = ((tile % per_chunk) * 4 + t) * pieces + piece
                stat[tile // per_chunk, owner % 2, owner // 2] += term[:, piece * span:(piece + 1) * span]
            q_part = q_half[:, pl.ds(start, WORD_BLOCK)]
            sum_a = product(q_part, ratio_a, 1, 0)
            sum_b = product(q_part, ratio_b, 1, 0)
            if tile == 0 and t == 0:
                allele[block, 0] = sum_a
                allele[block, 1] = sum_b
            else:
                allele[block, 0] += sum_a
                allele[block, 1] += sum_b

    def own_rows(spot):
        return pl.ds(pl.multiple_of(side * side_rows + spot * rows, rows), rows)

    def half_copy(block):
        other = pl.ds(pl.multiple_of((1 - side) * side_rows, side_rows), side_rows)
        return remote(
            allele.at[block, :, other], allele_one.at[block], half_send, half_recv, block, neighbour
        )

    def allele_copy(block, step):
        return remote(
            allele.at[block, :, own_rows(level_peer(step))], allele_two.at[block, step - 1],
            allele_send, allele_recv, (block, step - 1), level_id(step),
        )

    def block_columns(block):
        start = block * SNP_BLOCK
        if not isinstance(start, int):
            start = pl.multiple_of(start, SNP_BLOCK)
        return pl.ds(start, SNP_BLOCK)

    def fresh_place(block, spot):
        return freq_out.at[own_rows(spot), block_columns(block)]

    def fresh_copy(block, step):
        return remote(
            fresh.at[block], fresh_place(block, level),
            fresh_send, fresh_recv, (block, step - 1), level_id(step),
        )

    def fresh_near(block):
        return remote(
            fresh.at[block], fresh_place(block, level),
            fresh_send, fresh_recv, (block, depth - 1), neighbour,
        )

    def fresh_keep(block):
        return pltpu.make_async_copy(fresh.at[block], fresh_place(block, level), fresh_own.at[block])

    def hand_copy(block, step):
        part = fresh_place(block, lax.rem(level + depth - step, depth))
        return remote(part, part, hand_send, hand_recv, (block, step - 1), neighbour)

    def allele_start(block):
        half_copy(block).start()

    def allele_pair(block):
        half_copy(block).wait()
        for step in range(1, depth):
            spot = level_peer(step)
            near = pl.ds(pl.multiple_of(spot * rows, rows), rows)
            allele[block, :, own_rows(spot), :] += allele_one[block, :, near, :]
            allele_copy(block, step).start()
        near = pl.ds(pl.multiple_of(level * rows, rows), rows)
        allele[block, :, own_rows(level), :] += allele_one[block, :, near, :]

    def allele_finish(block):
        total = allele[block, :, own_rows(level), :]
        for step in range(1, depth):
            allele_copy(block, step).wait_recv()
            total = total + allele_two[block, step - 1]
        current = freq_ref[own_rows(level), block_columns(block)]
        upper = current * total[0]
        fresh[block] = upper / (upper + (1.0 - current) * total[1])
        for step in range(1, depth):
            fresh_copy(block, step).start()
        fresh_near(block).start()
        fresh_keep(block).start()

    def allele_hand(block):
        for step in range(1, depth):
            fresh_copy(block, step).wait_recv()
            hand_copy(block, step).start()

    def direct_copy(step):
        peer = ind_peer(step)
        start = lax.rem(peer, 2) * side_rows + peer // 2 * rows
        return remote(
            allele.at[last, :, pl.ds(pl.multiple_of(start, rows), rows)], allele_in.at[step - 1],
            direct_send, direct_recv, step - 1, {"ind": peer},
        )

    def last_copy(step):
        return remote(
            fresh.at[last], fresh_place(last, level),
            last_send, last_recv, step - 1, {"ind": ind_peer(step)},
        )

    def direct_finish():
        total = allele[last, :, own_rows(level), :]
        for step in range(1, n_ind):
            direct_copy(step).wait_recv()
            total = total + allele_in[step - 1]
        current = freq_ref[own_rows(level), block_columns(last)]
        upper = current * total[0]
        fresh[last] = upper / (upper + (1.0 - current) * total[1])
        for step in range(1, n_ind):
            last_copy(step).start()
        fresh_keep(last).start()

    def one_copy(chunk):
        return remote(
            stat.at[chunk, 1 - core], stat_one.at[chunk], one_send, one_recv, chunk, mate
        )

    def two_copy(chunk, step):
        return remote(
            stat.at[chunk, core, place_peer(step)], stat_two.at[chunk, step - 1],
            two_send, two_recv, (chunk, step - 1), place_id(step),
        )

    def individuals(chunk, owner):
        run = owner // pieces
        tile = chunk * per_chunk + run // 4
        start = lax.rem(run, 4) * height + tile * WORD_BLOCK + lax.rem(owner, pieces) * span
        return pl.ds(pl.multiple_of(start, span), span)

    def new_copy(chunk, step):
        return remote(
            updated.at[chunk], anc_out.at[:, individuals(chunk, here)],
            new_send, new_recv, (chunk, step - 1), place_id(step),
        )

    def new_mate(chunk):
        return remote(
            updated.at[chunk], anc_out.at[:, individuals(chunk, here)],
            new_send, new_recv, (chunk, half - 1), mate,
        )

    def new_keep(chunk):
        return pltpu.make_async_copy(
            updated.at[chunk], anc_out.at[:, individuals(chunk, here)], own_sem.at[chunk]
        )

    def pass_copy(chunk, step):
        owner = lax.rem(place + half - step, half) * 2 + core
        part = anc_out.at[:, individuals(chunk, owner)]
        return remote(part, part, pass_send, pass_recv, (chunk, step - 1), mate)

    def stat_send(chunk):
        one_copy(chunk).start()

    def stat_pair(chunk):
        one_copy(chunk).wait()
        for step in range(1, half):
            peer = place_peer(step)
            stat[chunk, core, peer] += stat_one[chunk, peer]
            two_copy(chunk, step).start()
        stat[chunk, core, place] += stat_one[chunk, place]

    def stat_new(chunk):
        total = stat[chunk, core, place]
        for step in range(1, half):
            two_copy(chunk, step).wait_recv()
            total = total + stat_two[chunk, step - 1]
        weighted = anc_ref[:, individuals(chunk, here)] * total
        updated[chunk] = k * weighted / jnp.sum(weighted, axis=0, keepdims=True)
        for step in range(1, half):
            new_copy(chunk, step).start()
        new_mate(chunk).start()
        new_keep(chunk).start()

    def stat_pass(chunk):
        for step in range(1, half):
            new_copy(chunk, step).wait_recv()
            pass_copy(chunk, step).start()

    stages = (stat_send, stat_pair, stat_new, stat_pass)

    def tick(now):
        for stage, act in enumerate(stages):
            if 0 <= now - stage < chunks:
                act(now - stage)

    def sweep(block, carry):
        for tile in range(tiles):
            tile_terms(block, tile)

        @pl.when(block == 0)
        def _():
            pl.semaphore_wait(barrier, n_ind - 1 + half)

        allele_start(block)

        @pl.when(block > 0)
        def _():
            allele_pair(block - 1)

        @pl.when(block > 1)
        def _():
            allele_finish(block - 2)

        return carry

    lax.fori_loop(0, last, sweep, 0)
    for tile in range(tiles):
        tile_terms(last, tile)
        if tile == tiles - 2:
            allele_pair(last - 1)
            allele_finish(last - 2)
            for block in range(last - 2):
                allele_hand(block)
        if tile == tiles - 1:
            for step in range(1, n_ind):
                direct_copy(step).start()
        if (tile + 1) % per_chunk == 0:
            tick(tile // per_chunk)
    end = chunks - 1
    stat_pair(end)
    if end > 1:
        stat_pass(end - 2)
    stat_new(end - 1)
    allele_finish(last - 1)
    allele_hand(last - 2)
    stat_new(end)
    stat_pass(end - 1)
    direct_finish()
    allele_hand(last - 1)
    stat_pass(end)

    for chunk in range(chunks):
        for step in range(1, half):
            two_copy(chunk, step).wait_send()
            new_copy(chunk, step).wait_send()
            pass_copy(chunk, step).wait()
        new_mate(chunk).wait()
        new_keep(chunk).wait()
    for block in range(last):
        for step in range(1, depth):
            allele_copy(block, step).wait_send()
            fresh_copy(block, step).wait_send()
            hand_copy(block, step).wait()
        fresh_near(block).wait()
        fresh_keep(block).wait()
    for step in range(1, n_ind):
        direct_copy(step).wait_send()
        last_copy(step).wait()
    fresh_keep(last).wait()


def on_device(n_ind, n_snp, genotypes, ancestry, frequency):
    k, people = ancestry.shape
    columns = frequency.shape[1]
    height = genotypes.shape[0]
    blocks = columns // SNP_BLOCK
    tiles = height // WORD_BLOCK
    half = n_snp // 2
    depth = n_ind // 2
    chunks = min(tiles, people // (n_snp * 128))
    span = people // (chunks * n_snp)
    rows = k // n_ind
    dma = pltpu.SemaphoreType.DMA
    vmem = pl.BlockSpec(memory_space=pltpu.VMEM)
    anywhere = pl.BlockSpec(memory_space=pl.ANY)
    return pl.pallas_call(
        functools.partial(kernel, n_ind, n_snp, chunks),
        out_shape=(
            jax.ShapeDtypeStruct(ancestry.shape, F32),
            jax.ShapeDtypeStruct(frequency.shape, F32),
        ),
        in_specs=[anywhere, vmem, vmem],
        out_specs=(anywhere, anywhere),
        scratch_shapes=[
            pltpu.VMEM((blocks, height, SNP_BLOCK), jnp.int32),
            pltpu.VMEM((k, people), BF16),
            pltpu.VMEM((people, k), BF16),
            pltpu.VMEM((blocks, k, SNP_BLOCK), BF16),
            pltpu.VMEM((blocks, k, SNP_BLOCK), BF16),
            pltpu.VMEM((blocks, 2, k, SNP_BLOCK), F32),
            pltpu.VMEM((blocks, 2, k // 2, SNP_BLOCK), F32),
            pltpu.VMEM((blocks, depth - 1, 2, rows, SNP_BLOCK), F32),
            pltpu.VMEM((n_ind - 1, 2, rows, SNP_BLOCK), F32),
            pltpu.VMEM((blocks, rows, SNP_BLOCK), F32),
            pltpu.VMEM((chunks, 2, half, k, span), F32),
            pltpu.VMEM((chunks, half, k, span), F32),
            pltpu.VMEM((chunks, half - 1, k, span), F32),
            pltpu.VMEM((chunks, k, span), F32),
            dma((blocks, tiles)),
            dma((blocks,)),
            dma((blocks,)),
            dma((blocks, depth - 1)),
            dma((blocks, depth - 1)),
            dma((blocks, depth)),
            dma((blocks, depth)),
            dma((blocks,)),
            dma((blocks, depth - 1)),
            dma((blocks, depth - 1)),
            dma((n_ind - 1,)),
            dma((n_ind - 1,)),
            dma((n_ind - 1,)),
            dma((n_ind - 1,)),
            dma((chunks,)),
            dma((chunks,)),
            dma((chunks, half - 1)),
            dma((chunks, half - 1)),
            dma((chunks, half)),
            dma((chunks, half)),
            dma((chunks, half - 1)),
            dma((chunks, half - 1)),
            dma((chunks,)),
        ],
        compiler_params=pltpu.CompilerParams(
            collective_id=0, has_side_effects=True, vmem_limit_bytes=48 * 2**20
        ),
        name="admixture_step",
    )(genotypes, ancestry, frequency)


def solution(mesh):
    placed = (P(("group", "ind"), "snp"), P(None, ("group", "ind")), P(None, ("group", "snp")))
    return jax.shard_map(
        functools.partial(on_device, mesh.shape["ind"], mesh.shape["snp"]),
        mesh=mesh,
        in_specs=placed,
        out_specs=(P(None, ("group", "ind")), P(None, ("group", "snp"))),
        check_vma=False,
    )
```

```python
import functools

import jax
import jax.numpy as jnp
from jax import lax
from jax.experimental import pallas as pl
from jax.experimental.pallas import tpu as pltpu
from jax.sharding import PartitionSpec as P

F32 = jnp.float32
BF16 = jnp.bfloat16
SNP_BLOCK = 512
WORD_BLOCK = 256
MESH = pl.DeviceIdType.MESH


def product(left, right, left_dim, right_dim):
    return lax.dot_general(
        left, right, (((left_dim,), (right_dim,)), ((), ())), preferred_element_type=F32
    )


def remote(src, dst, sems, recv, index, target):
    return pltpu.make_async_remote_copy(
        src_ref=src,
        dst_ref=dst,
        send_sem=sems.at[index],
        recv_sem=recv.at[index],
        device_id=target,
        device_id_type=MESH,
    )


def kernel(
    n_ind, n_snp, chunks,
    words_ref, anc_ref, freq_ref, anc_out, freq_out,
    words, q_half, q_turned, f_half, rest_half, allele, allele_one, allele_two, allele_in, fresh,
    stat, stat_one, stat_two, updated,
    word_sem, half_send, half_recv, allele_send, allele_recv, fresh_send, fresh_recv, fresh_own,
    hand_send, hand_recv, direct_send, direct_recv, last_send, last_recv,
    one_send, one_recv, two_send, two_recv, new_send, new_recv, pass_send, pass_recv, own_sem,
):
    k, people = anc_ref.shape
    columns = freq_ref.shape[1]
    height = words_ref.shape[0]
    blocks = columns // SNP_BLOCK
    tiles = height // WORD_BLOCK
    last = blocks - 1
    rows = k // n_ind
    half = n_snp // 2
    depth = n_ind // 2
    side_rows = k // 2
    span = people // (chunks * n_snp)
    pieces = WORD_BLOCK // span
    per_chunk = tiles // chunks

    me = lax.axis_index("ind")
    side = lax.rem(me, 2)
    level = me // 2
    neighbour = {"ind": me + 1 - 2 * side}
    here = lax.axis_index("snp")
    core = lax.rem(here, 2)
    place = here // 2
    mate = {"snp": here + 1 - 2 * core}

    def ind_peer(step):
        return lax.rem(me + step, n_ind)

    def level_peer(step):
        return lax.rem(level + step, depth)

    def level_id(step):
        return {"ind": level_peer(step) * 2 + side}

    def place_peer(step):
        return lax.rem(place + step, half)

    def place_id(step):
        return {"snp": place_peer(step) * 2 + core}

    def word_copy(block, tile):
        start = block * SNP_BLOCK
        if not isinstance(start, int):
            start = pl.multiple_of(start, SNP_BLOCK)
        return pltpu.make_async_copy(
            words_ref.at[pl.ds(tile * WORD_BLOCK, WORD_BLOCK), pl.ds(start, SNP_BLOCK)],
            words.at[block, pl.ds(tile * WORD_BLOCK, WORD_BLOCK)],
            word_sem.at[block, tile],
        )

    for block in range(blocks):
        for tile in range(tiles):
            word_copy(block, tile).start()

    barrier = pltpu.get_barrier_semaphore()
    for step in range(1, n_ind):
        pl.semaphore_signal(barrier, 1, device_id={"ind": ind_peer(step)}, device_id_type=MESH)
    for step in range(1, half):
        pl.semaphore_signal(barrier, 1, device_id=place_id(step), device_id_type=MESH)
    pl.semaphore_signal(barrier, 1, device_id=mate, device_id_type=MESH)

    for block in range(blocks):
        cols = pl.ds(block * SNP_BLOCK, SNP_BLOCK)
        f_part = freq_ref[:, cols]
        f_half[block] = f_part.astype(BF16)
        rest_half[block] = (1.0 - f_part).astype(BF16)
    for run in range(people // WORD_BLOCK):
        cols = pl.ds(run * WORD_BLOCK, WORD_BLOCK)
        part = anc_ref[:, cols].astype(BF16)
        q_half[:, cols] = part
        q_turned[cols, :] = part.T
    stat[...] = jnp.zeros_like(stat)

    def tile_terms(block, tile):
        word_copy(block, tile).wait()
        f_part = f_half[block]
        rest_part = rest_half[block]
        packed = words[block, pl.ds(tile * WORD_BLOCK, WORD_BLOCK), :].astype(jnp.int16)
        for t in range(4):
            start = t * height + tile * WORD_BLOCK
            mixed = product(q_turned[pl.ds(start, WORD_BLOCK), :], f_part, 1, 0)
            inv_a = pltpu.reciprocal(mixed, approx=True).astype(BF16)
            inv_b = pltpu.reciprocal(1.0 - mixed, approx=True).astype(BF16)
            code = packed & jnp.int16(3 << (2 * t))
            one = code == jnp.int16(1 << (2 * t))
            two = code == jnp.int16(2 << (2 * t))
            none = code == jnp.int16(0)
            zero = jnp.zeros_like(inv_a)
            ratio_a = jnp.where(one, inv_a, jnp.where(two, inv_a + inv_a, zero))
            ratio_b = jnp.where(one, inv_b, jnp.where(none, inv_b + inv_b, zero))
            term = product(f_part, ratio_a, 1, 1) + product(rest_part, ratio_b, 1, 1)
            for piece in range(pieces):
                owner = ((tile % per_chunk) * 4 + t) * pieces + piece
                stat[tile // per_chunk, owner % 2, owner // 2] += term[:, piece * span:(piece + 1) * span]
            q_part = q_half[:, pl.ds(start, WORD_BLOCK)]
            sum_a = product(q_part, ratio_a, 1, 0)
            sum_b = product(q_part, ratio_b, 1, 0)
            if tile == 0 and t == 0:
                allele[block, 0] = sum_a
                allele[block, 1] = sum_b
            else:
                allele[block, 0] += sum_a
                allele[block, 1] += sum_b

    def own_rows(spot):
        return pl.ds(pl.multiple_of(side * side_rows + spot * rows, rows), rows)

    def half_copy(block):
        other = pl.ds(pl.multiple_of((1 - side) * side_rows, side_rows), side_rows)
        return remote(
            allele.at[block, :, other], allele_one.at[block], half_send, half_recv, block, neighbour
        )

    def allele_copy(block, step):
        return remote(
            allele.at[block, :, own_rows(level_peer(step))], allele_two.at[block, step - 1],
            allele_send, allele_recv, (block, step - 1), level_id(step),
        )

    def block_columns(block):
        start = block * SNP_BLOCK
        if not isinstance(start, int):
            start = pl.multiple_of(start, SNP_BLOCK)
        return pl.ds(start, SNP_BLOCK)

    def fresh_place(block, spot):
        return freq_out.at[own_rows(spot), block_columns(block)]

    def fresh_copy(block, step):
        return remote(
            fresh.at[block], fresh_place(block, level),
            fresh_send, fresh_recv, (block, step - 1), level_id(step),
        )

    def fresh_near(block):
        return remote(
            fresh.at[block], fresh_place(block, level),
            fresh_send, fresh_recv, (block, depth - 1), neighbour,
        )

    def fresh_keep(block):
        return pltpu.make_async_copy(fresh.at[block], fresh_place(block, level), fresh_own.at[block])

    def hand_copy(block, step):
        part = fresh_place(block, lax.rem(level + depth - step, depth))
        return remote(part, part, hand_send, hand_recv, (block, step - 1), neighbour)

    def allele_start(block):
        half_copy(block).start()

    def allele_pair(block):
        half_copy(block).wait()
        for step in range(1, depth):
            spot = level_peer(step)
            near = pl.ds(pl.multiple_of(spot * rows, rows), rows)
            allele[block, :, own_rows(spot), :] += allele_one[block, :, near, :]
            allele_copy(block, step).start()
        near = pl.ds(pl.multiple_of(level * rows, rows), rows)
        allele[block, :, own_rows(level), :] += allele_one[block, :, near, :]

    def allele_finish(block):
        total = allele[block, :, own_rows(level), :]
        for step in range(1, depth):
            allele_copy(block, step).wait_recv()
            total = total + allele_two[block, step - 1]
        current = freq_ref[own_rows(level), block_columns(block)]
        upper = current * total[0]
        fresh[block] = upper / (upper + (1.0 - current) * total[1])
        for step in range(1, depth):
            fresh_copy(block, step).start()
        fresh_near(block).start()
        fresh_keep(block).start()

    def allele_hand(block):
        for step in range(1, depth):
            fresh_copy(block, step).wait_recv()
            hand_copy(block, step).start()

    def direct_copy(step):
        peer = ind_peer(step)
        start = lax.rem(peer, 2) * side_rows + peer // 2 * rows
        return remote(
            allele.at[last, :, pl.ds(pl.multiple_of(start, rows), rows)], allele_in.at[step - 1],
            direct_send, direct_recv, step - 1, {"ind": peer},
        )

    def last_copy(step):
        return remote(
            fresh.at[last], fresh_place(last, level),
            last_send, last_recv, step - 1, {"ind": ind_peer(step)},
        )

    def direct_finish():
        total = allele[last, :, own_rows(level), :]
        for step in range(1, n_ind):
            direct_copy(step).wait_recv()
            total = total + allele_in[step - 1]
        current = freq_ref[own_rows(level), block_columns(last)]
        upper = current * total[0]
        fresh[last] = upper / (upper + (1.0 - current) * total[1])
        for step in range(1, n_ind):
            last_copy(step).start()
        fresh_keep(last).start()

    def one_copy(chunk):
        return remote(
            stat.at[chunk, 1 - core], stat_one.at[chunk], one_send, one_recv, chunk, mate
        )

    def two_copy(chunk, step):
        return remote(
            stat.at[chunk, core, place_peer(step)], stat_two.at[chunk, step - 1],
            two_send, two_recv, (chunk, step - 1), place_id(step),
        )

    def individuals(chunk, owner):
        run = owner // pieces
        tile = chunk * per_chunk + run // 4
        start = lax.rem(run, 4) * height + tile * WORD_BLOCK + lax.rem(owner, pieces) * span
        return pl.ds(pl.multiple_of(start, span), span)

    def new_copy(chunk, step):
        return remote(
            updated.at[chunk], anc_out.at[:, individuals(chunk, here)],
            new_send, new_recv, (chunk, step - 1), place_id(step),
        )

    def new_mate(chunk):
        return remote(
            updated.at[chunk], anc_out.at[:, individuals(chunk, here)],
            new_send, new_recv, (chunk, half - 1), mate,
        )

    def new_keep(chunk):
        return pltpu.make_async_copy(
            updated.at[chunk], anc_out.at[:, individuals(chunk, here)], own_sem.at[chunk]
        )

    def pass_copy(chunk, step):
        owner = lax.rem(place + half - step, half) * 2 + core
        part = anc_out.at[:, individuals(chunk, owner)]
        return remote(part, part, pass_send, pass_recv, (chunk, step - 1), mate)

    def stat_send(chunk):
        one_copy(chunk).start()

    def stat_pair(chunk):
        one_copy(chunk).wait()
        for step in range(1, half):
            peer = place_peer(step)
            stat[chunk, core, peer] += stat_one[chunk, peer]
            two_copy(chunk, step).start()
        stat[chunk, core, place] += stat_one[chunk, place]

    def stat_new(chunk):
        total = stat[chunk, core, place]
        for step in range(1, half):
            two_copy(chunk, step).wait_recv()
            total = total + stat_two[chunk, step - 1]
        weighted = anc_ref[:, individuals(chunk, here)] * total
        updated[chunk] = k * weighted / jnp.sum(weighted, axis=0, keepdims=True)
        for step in range(1, half):
            new_copy(chunk, step).start()
        new_mate(chunk).start()
        new_keep(chunk).start()

    def stat_pass(chunk):
        for step in range(1, half):
            new_copy(chunk, step).wait_recv()
            pass_copy(chunk, step).start()

    stages = (stat_send, stat_pair, stat_new, stat_pass)

    def tick(now):
        for stage, act in enumerate(stages):
            if 0 <= now - stage < chunks:
                act(now - stage)

    def sweep(block, carry):
        for tile in range(tiles):
            tile_terms(block, tile)

        @pl.when(block == 0)
        def _():
            pl.semaphore_wait(barrier, n_ind - 1 + half)

        allele_start(block)

        @pl.when(block > 0)
        def _():
            allele_pair(block - 1)

        @pl.when(block > 1)
        def _():
            allele_finish(block - 2)

        return carry

    lax.fori_loop(0, last, sweep, 0)
    for tile in range(tiles):
        tile_terms(last, tile)
        if tile == tiles - 2:
            allele_pair(last - 1)
            allele_finish(last - 2)
            for block in range(last - 2):
                allele_hand(block)
        if tile == tiles - 1:
            for step in range(1, n_ind):
                direct_copy(step).start()
        if (tile + 1) % per_chunk == 0:
            tick(tile // per_chunk)
    end = chunks - 1
    stat_pair(end)
    if end > 1:
        stat_pass(end - 2)
    allele_finish(last - 1)
    stat_new(end - 1)
    stat_new(end)
    direct_finish()
    allele_hand(last - 2)
    stat_pass(end - 1)
    allele_hand(last - 1)
    stat_pass(end)

    for chunk in range(chunks):
        for step in range(1, half):
            two_copy(chunk, step).wait_send()
            new_copy(chunk, step).wait_send()
            pass_copy(chunk, step).wait()
        new_mate(chunk).wait()
        new_keep(chunk).wait()
    for block in range(last):
        for step in range(1, depth):
            allele_copy(block, step).wait_send()
            fresh_copy(block, step).wait_send()
            hand_copy(block, step).wait()
        fresh_near(block).wait()
        fresh_keep(block).wait()
    for step in range(1, n_ind):
        direct_copy(step).wait_send()
        last_copy(step).wait()
    fresh_keep(last).wait()


def on_device(n_ind, n_snp, genotypes, ancestry, frequency):
    k, people = ancestry.shape
    columns = frequency.shape[1]
    height = genotypes.shape[0]
    blocks = columns // SNP_BLOCK
    tiles = height // WORD_BLOCK
    half = n_snp // 2
    depth = n_ind // 2
    chunks = min(tiles, people // (n_snp * 128))
    span = people // (chunks * n_snp)
    rows = k // n_ind
    dma = pltpu.SemaphoreType.DMA
    vmem = pl.BlockSpec(memory_space=pltpu.VMEM)
    anywhere = pl.BlockSpec(memory_space=pl.ANY)
    return pl.pallas_call(
        functools.partial(kernel, n_ind, n_snp, chunks),
        out_shape=(
            jax.ShapeDtypeStruct(ancestry.shape, F32),
            jax.ShapeDtypeStruct(frequency.shape, F32),
        ),
        in_specs=[anywhere, vmem, vmem],
        out_specs=(anywhere, anywhere),
        scratch_shapes=[
            pltpu.VMEM((blocks, height, SNP_BLOCK), jnp.int32),
            pltpu.VMEM((k, people), BF16),
            pltpu.VMEM((people, k), BF16),
            pltpu.VMEM((blocks, k, SNP_BLOCK), BF16),
            pltpu.VMEM((blocks, k, SNP_BLOCK), BF16),
            pltpu.VMEM((blocks, 2, k, SNP_BLOCK), F32),
            pltpu.VMEM((blocks, 2, k // 2, SNP_BLOCK), F32),
            pltpu.VMEM((blocks, depth - 1, 2, rows, SNP_BLOCK), F32),
            pltpu.VMEM((n_ind - 1, 2, rows, SNP_BLOCK), F32),
            pltpu.VMEM((blocks, rows, SNP_BLOCK), F32),
            pltpu.VMEM((chunks, 2, half, k, span), F32),
            pltpu.VMEM((chunks, half, k, span), F32),
            pltpu.VMEM((chunks, half - 1, k, span), F32),
            pltpu.VMEM((chunks, k, span), F32),
            dma((blocks, tiles)),
            dma((blocks,)),
            dma((blocks,)),
            dma((blocks, depth - 1)),
            dma((blocks, depth - 1)),
            dma((blocks, depth)),
            dma((blocks, depth)),
            dma((blocks,)),
            dma((blocks, depth - 1)),
            dma((blocks, depth - 1)),
            dma((n_ind - 1,)),
            dma((n_ind - 1,)),
            dma((n_ind - 1,)),
            dma((n_ind - 1,)),
            dma((chunks,)),
            dma((chunks,)),
            dma((chunks, half - 1)),
            dma((chunks, half - 1)),
            dma((chunks, half)),
            dma((chunks, half)),
            dma((chunks, half - 1)),
            dma((chunks, half - 1)),
            dma((chunks,)),
        ],
        compiler_params=pltpu.CompilerParams(
            collective_id=0, has_side_effects=True, vmem_limit_bytes=48 * 2**20
        ),
        name="admixture_step",
    )(genotypes, ancestry, frequency)


def solution(mesh):
    placed = (P(("group", "ind"), "snp"), P(None, ("group", "ind")), P(None, ("group", "snp")))
    return jax.shard_map(
        functools.partial(on_device, mesh.shape["ind"], mesh.shape["snp"]),
        mesh=mesh,
        in_specs=placed,
        out_specs=(P(None, ("group", "ind")), P(None, ("group", "snp"))),
        check_vma=False,
    )
```
